512 devices in a mesh: hist: 64 (over z_lo, x, y), dom: 8 (over z_hi, core).
Axes of the slice: x: 4, y: 4, z: 16 (z_hi: 4, z_lo: 4; z = z_hi * 4 + z_lo), core: 2. Of those that a mesh axis runs over, the one named last changes fastest.
Arguments:
- coords: float32 [6, 1048576], P(None, ('dom', 'hist')), may hold values from -3 to 3
- charge: float32 [1048576], P(('dom', 'hist')), may hold values from 0.02 to 0.2
- row_index: int32 [1048576], P(('dom', 'hist')), may hold values from 0 to 511, as said below
- block_col: int32 [8192], P(('dom', 'hist')), may hold values from 0 to 496
- col_offset: int32 [1048576], P(('dom', 'hist')), may hold values from 0 to 15
- transfer_map: float32 [6, 84], replicated
- history: bfloat16 [512, 2, 512, 512], P('hist', None, 'dom'), may hold values from -16 to 16
- retard_index: int32 [512], P('hist'), may hold values from 0 to 16
- retard_frac: float32 [512], P('hist'), may hold values from 0 to 1
- retard_weight: float32 [512], P('hist'), may hold values from 0.005 to 0.05
- z_kernel: float32 [512, 512], P(None, 'dom')
- x_kernel: float32 [512, 512], replicated
Outputs:
- kicked: float32 [6, 1048576], P(None, ('dom', 'hist'))
- field: float32 [2, 512, 512], P(None, 'dom', 'hist')
- deposit: float32 [2, 512, 512], P(None, 'dom', 'hist')
The draws below stay inside these ranges and needn't reach their ends.
Inputs may be any that keep to these rules, and one draw needn't show every extreme that they name: `row_index`: particle i lies in grid slab i // (1048576 // 8): its row is that slab's number times 64 plus 0 to 63.
All inputs are finite; a program needn't handle non-finite values.
Results may differ from the reference program's by a relative error of at most 0.0019.
Values may be sent and summed in bfloat16 or wider, within the bound.
A program may use at most 64 MiB of HBM per device.

```python
import math
import jax
import jax.numpy as jnp
from jax import lax

NR = 512
NC = 512
P_DEV = 2048
BLOCK = 128
COLW = 16
KMAX = 16
SLAB = 64
NT = 512
PARTICLES = 1048576
NBLOCKS = 8192
N_DOM = 8


def draw_row_index(key, part):
    index = jnp.arange(PARTICLES, dtype=jnp.int32)
    slab_number = index // (PARTICLES // N_DOM)
    within = jax.random.randint(key, (PARTICLES,), 0, SLAB, dtype=jnp.int32)
    return (slab_number * SLAB + within).astype(jnp.int32)


def kernel_draw(key, order):
    noise = jax.random.normal(key, (order, order), jnp.float32)
    identity = (jnp.arange(order)[:, None] == jnp.arange(order)[None, :]).astype(jnp.float32)
    return identity + 0.5 * noise / jnp.sqrt(jnp.float32(order))


def draw_z_kernel(key, part):
    return kernel_draw(jax.random.fold_in(key, 11), NR)


def draw_x_kernel(key, part):
    return kernel_draw(jax.random.fold_in(key, 23), NC)


def draw_transfer_map(key, part):
    noise = 0.05 * jax.random.normal(key, (6, 84), jnp.float32)
    linear = (jnp.arange(84)[None, :] == jnp.arange(6)[:, None] + 1).astype(jnp.float32)
    return linear + noise


def set_ends(drawn, own_key, low, top_value):
    longest = drawn.shape.index(max(drawn.shape))
    spots = []
    for shift in (0, 1):
        where = [jax.random.randint(jax.random.fold_in(own_key, axis), (), 0, length) for axis, length in enumerate(drawn.shape)]
        where[longest] = (where[longest] + shift) % drawn.shape[longest]
        spots.append(tuple(where))
    return drawn.at[spots[0]].set(low).at[spots[1]].set(top_value)


def spiked(values, own_key, source, target, blocks, factor):
    owner, partner = [(jnp.arange(values.shape[dim]) // (values.shape[dim] // blocks)).reshape([-1 if axis == dim else 1 for axis in range(values.ndim)]) for dim in (source, target)]
    chosen = jax.random.permutation(own_key, blocks)[partner]
    strong = (owner == chosen) | (owner == (partner + blocks // 2) % blocks)
    return jnp.where(strong, factor * values, values)


def shard_levels(stream_key, shape, pieces, low, top_value):
    gain = 1.0
    for axis_at, blocks in pieces:
        heights = jax.random.uniform(jax.random.fold_in(jax.random.fold_in(stream_key, 6), axis_at), (blocks,), jnp.float32, low / len(pieces), top_value / len(pieces))
        gain = gain * jnp.repeat(jnp.exp(heights), shape[axis_at] // blocks).reshape((-1,) + (1,) * (len(shape) - 1 - axis_at))
    return gain


def normal_values(rng, extent, deviation, limit, pieces=(), kind=jnp.bfloat16):
    drawn = deviation * jax.random.normal(rng, extent, jnp.float32)
    if pieces:
        drawn = drawn * shard_levels(rng, extent, pieces, -0.22, 0.18)
    return jnp.clip(drawn, -limit, limit).astype(kind)


def gaussian_with(rng, dims, spread, bound, shards, heavy, kind=jnp.bfloat16):
    drawn = spread * jax.random.normal(rng, dims, jnp.float32)
    if shards:
        drawn = drawn * shard_levels(rng, dims, shards, -0.22, 0.18)
    return jnp.clip(spiked(drawn, jax.random.fold_in(rng, 3), *heavy), -bound, bound).astype(kind)


def setup_inputs(seed: int = 0) -> dict:
    splits = jax.random.split(jax.random.key(seed), 13)
    return {
        "coords": normal_values(splits[0], (6, PARTICLES), 1.0, 3.0, ((1, 512),), jnp.float32),
        "charge": jnp.clip(jnp.exp(math.log(0.2) - 2.3025851 * jax.random.uniform(splits[1], (PARTICLES,), jnp.float32) ** shard_levels(splits[1], (PARTICLES,), ((0, 512),), -0.2, 0.2)), 0.02, 0.2),
        "row_index": draw_row_index(jax.random.fold_in(splits[12], 71), 0),
        "block_col": set_ends(jax.random.randint(splits[3], (NBLOCKS,), 0, NC - COLW + 1), jax.random.fold_in(splits[3], 1), 0, NC - COLW).astype(jnp.int32),
        "col_offset": set_ends(jax.random.randint(splits[4], (PARTICLES,), 0, COLW), jax.random.fold_in(splits[4], 1), 0, COLW - 1).astype(jnp.int32),
        "transfer_map": draw_transfer_map(jax.random.fold_in(splits[12], 71), 0),
        "history": gaussian_with(splits[6], (NT, 2, NR, NC), 1.0, 16.0, ((0, 64), (2, 8)), (0, 3, 64, 4.0)),
        "retard_index": set_ends(jax.random.randint(splits[7], (NT,), 0, KMAX + 1), jax.random.fold_in(splits[7], 1), 0, KMAX).astype(jnp.int32),
        "retard_frac": jnp.clip(1.0 * jax.random.uniform(splits[8], (NT,), jnp.float32) ** shard_levels(splits[8], (NT,), ((0, 64),), -0.2, 0.2), 0.0, 1.0),
        "retard_weight": jnp.clip(jnp.exp(math.log(0.05) - 2.3025851 * jax.random.uniform(splits[9], (NT,), jnp.float32) ** shard_levels(splits[9], (NT,), ((0, 64),), -0.2, 0.2)), 0.005, 0.05),
        "z_kernel": draw_z_kernel(jax.random.fold_in(splits[12], 71), 0),
        "x_kernel": draw_x_kernel(jax.random.fold_in(splits[12], 71), 0),
    }


def monomials(coords):
    products = [jnp.ones_like(coords[0])]
    for first in range(6):
        products.append(coords[first])
    for first in range(6):
        for second in range(first, 6):
            products.append(coords[first] * coords[second])
    for first in range(6):
        for second in range(first, 6):
            for third in range(second, 6):
                products.append(coords[first] * coords[second] * coords[third])
    return jnp.stack(products)


def retarded_source(history, retard_index, retard_frac, retard_weight):
    count_steps, comps, rows_here, width = history.shape

    def add_step(position, total):
        frame = lax.dynamic_index_in_dim(history, position, 0, keepdims=False).astype(jnp.float32)
        padded = jnp.pad(frame, ((0, 0), (0, 0), (width + 1, 0)))
        lag = retard_index[position].astype(jnp.int32)
        near = lax.dynamic_slice_in_dim(padded, (width + 1 - lag).astype(jnp.int32), width, 2)
        far = lax.dynamic_slice_in_dim(padded, (width - lag).astype(jnp.int32), width, 2)
        fraction = retard_frac[position]
        return total + retard_weight[position] * ((1.0 - fraction) * near + fraction * far)

    start = jnp.zeros((comps, rows_here, width), jnp.float32)
    return lax.fori_loop(0, count_steps, add_step, start)


def reference(coords, charge, row_index, block_col, col_offset, transfer_map, history, retard_index, retard_frac, retard_weight, z_kernel, x_kernel):
    highest = lax.Precision.HIGHEST
    grouped = coords.reshape(6, -1, P_DEV).transpose(1, 0, 2)

    def push_group(group_coords):
        return jnp.dot(transfer_map, monomials(group_coords), precision=highest)

    pushed = lax.map(push_group, grouped).transpose(1, 0, 2).reshape(6, -1)
    column = (jnp.repeat(block_col, BLOCK) + col_offset).astype(jnp.int32)
    weights = jnp.stack([charge, charge * pushed[1]]).astype(jnp.bfloat16)
    weights = lax.optimization_barrier(weights).astype(jnp.float32)
    flat = (row_index * NC + column).astype(jnp.int32)
    deposit = jnp.zeros((2, NR * NC), jnp.float32).at[:, flat].add(weights).reshape(2, NR, NC)
    source = retarded_source(history, retard_index, retard_frac, retard_weight)
    field = jnp.einsum("rs,csx->crx", z_kernel, source, precision=highest)
    field = jnp.einsum("crx,xy->cry", field, x_kernel, precision=highest)
    rounded = lax.optimization_barrier(field.astype(jnp.bfloat16)).astype(jnp.float32)
    sampled = rounded[:, row_index, column]
    kicked = pushed.at[5].add(0.5 * sampled[0]).at[1].add(0.5 * sampled[1])
    return kicked, field, deposit
```

```python
import jax
import jax.numpy as jnp
from jax import lax
from jax.experimental import pallas as pl
from jax.experimental.pallas import tpu as pltpu
from jax.sharding import PartitionSpec as P

MESH = pl.DeviceIdType.MESH
F32 = jnp.float32
BF16 = jnp.bfloat16


def split(value):
    high = value.astype(BF16)
    return high, (value - high.astype(F32)).astype(BF16)


def dot_nn(a, b):
    return lax.dot_general(a, b, (((1,), (0,)), ((), ())), preferred_element_type=F32)


def dot_nt(a, b):
    return lax.dot_general(a, b, (((1,), (1,)), ((), ())), preferred_element_type=F32)


def dot_tn(a, b):
    return lax.dot_general(a, b, (((0,), (0,)), ((), ())), preferred_element_type=F32)


def kernel(
    coords_ref, charge_ref, row_ref, block_ref, offset_ref, map_ref, history_hbm, lag_ref, frac_ref,
    weight_ref, z_hbm, x_hbm,
    kicked_ref, field_ref, deposit_ref,
    history, x_full, z_own, near, far, x_high, x_low, z_high, z_low,
    a_send, a_recv, d_send, d_recv, e_send, e_recv, core_send, core_recv, ring_send, ring_recv,
    slab_t, column_hot, row_hot, pushed,
    load_sem, a_ssem, a_rsem, d_ssem, d_rsem, e_ssem, e_rsem, c_ssem, c_rsem, r_ssem, r_rsem,
    g_ssem, g_rsem,
):
    hist = lax.axis_index("hist")
    dom = lax.axis_index("dom")
    z_low_at, plane = hist // 16, hist % 16
    z_high_at, core = dom // 2, dom % 2
    z_at = z_high_at * 4 + z_low_at

    plane_peers = [{"hist": z_low_at * 16 + lax.rem(plane + k, 16), "dom": dom} for k in range(1, 16)]
    ring_at = [lax.rem(z_at + k, 16) for k in range(1, 16)]
    ring_peers = [{"hist": (at % 4) * 16 + plane, "dom": (at // 4) * 2 + core} for at in ring_at]
    low_at = [lax.rem(z_low_at + k, 4) for k in range(1, 4)]
    low_peers = [{"hist": at * 16 + plane, "dom": dom} for at in low_at]
    sibling = {"hist": hist, "dom": z_high_at * 2 + (1 - core)}

    load_history = pltpu.make_async_copy(history_hbm, history, load_sem.at[0])
    load_x = pltpu.make_async_copy(x_hbm, x_full, load_sem.at[1])
    load_z = pltpu.make_async_copy(z_hbm, z_own, load_sem.at[2])
    load_history.start()
    load_x.start()
    load_z.start()

    barrier = pltpu.get_barrier_semaphore()
    for peer in plane_peers + ring_peers + [sibling]:
        pl.semaphore_signal(barrier, inc=1, device_id=peer, device_id_type=MESH)

    lane = lax.broadcasted_iota(jnp.int32, (32, 128), 1)
    load_history.wait()

    def source_rows(group, carry):
        comp = group // 2
        row = pl.multiple_of((group % 2) * 32, 32)
        row_out = pl.multiple_of(group * 32, 32)
        near_sum = [jnp.zeros((32, 128), F32) for _ in range(4)]
        far_sum = [jnp.zeros((32, 128), F32) for _ in range(4)]
        for t in range(8):
            lag = lag_ref[t]
            fraction = frac_ref[t]
            weight = weight_ref[t]
            near_weight = weight * (1.0 - fraction)
            far_weight = weight * fraction
            inside = lane >= lag
            before = jnp.zeros((32, 128), F32)
            for j in range(4):
                piece = history[t, comp, pl.ds(row, 32), 128 * j : 128 * (j + 1)].astype(F32)
                turned = pltpu.roll(piece, lag, 1)
                moved = jnp.where(inside, turned, before)
                before = turned
                near_sum[j] = near_sum[j] + near_weight * moved
                far_sum[j] = far_sum[j] + far_weight * moved
        before = jnp.zeros((32, 128), F32)
        for j in range(4):
            turned = pltpu.roll(far_sum[j], 1, 1)
            near[pl.ds(row_out, 32), 128 * j : 128 * (j + 1)] = near_sum[j] + jnp.where(
                lane >= 1, turned, before
            )
            before = turned
        return carry

    lax.fori_loop(0, 4, source_rows, 0)

    load_x.wait()
    x_high[...], x_low[...] = split(x_full[...])
    s_high, s_low = split(near[...])
    twice = dot_nn(jnp.concatenate([s_high, s_low], axis=0), x_high[...])
    spread = twice[:128] + twice[128:] + dot_nn(s_high, x_low[...])
    spread_t = spread.T.reshape(4, 16, 8, 128)
    for zc in range(4):
        a_send[:, zc] = spread_t[zc]

    pl.semaphore_wait(barrier, 31)

    a_copies = []
    for k in range(1, 16):
        to = lax.rem(plane + k, 16)
        copy = pltpu.make_async_remote_copy(
            src_ref=a_send.at[to], dst_ref=a_recv.at[k - 1], send_sem=a_ssem.at[k - 1],
            recv_sem=a_rsem.at[k - 1], device_id=plane_peers[k - 1], device_id_type=MESH,
        )
        copy.start()
        a_copies.append(copy)

    load_z.wait()
    empty = jnp.zeros((64, 64), F32)
    for to in range(8):
        block = z_own[64 * to : 64 * (to + 1), :]
        pair = jnp.concatenate(
            [jnp.concatenate([block, empty], axis=1), jnp.concatenate([empty, block], axis=1)], axis=0
        )
        z_high[128 * to : 128 * (to + 1), :], z_low[128 * to : 128 * (to + 1), :] = split(pair)

    for chunk in range(4):
        lanes = slice(512 * chunk, 512 * (chunk + 1))
        wide = [jnp.broadcast_to(coords_ref[i : i + 1, lanes], (6, 512)) for i in range(6)]
        total = jnp.broadcast_to(map_ref[:, 0:1], (6, 512))
        at = 1
        for i in range(6):
            total = total + map_ref[:, at : at + 1] * wide[i]
            at += 1
        for i in range(6):
            for j in range(i, 6):
                total = total + map_ref[:, at : at + 1] * (wide[i] * wide[j])
                at += 1
        for i in range(6):
            for j in range(i, 6):
                two = wide[i] * wide[j]
                for k in range(j, 6):
                    total = total + map_ref[:, at : at + 1] * (two * wide[k])
                    at += 1
        pushed[:, lanes] = total

    row = row_ref[...] - dom * 64
    first = jnp.concatenate([jnp.full((1, 128), block_ref[b], jnp.int32) for b in range(16)], axis=1)
    column = first + offset_ref[...]
    place = ((column >> 3) & 15) * 32 + (column >> 7) * 8 + (column & 7)
    charge = charge_ref[...]
    weights = [charge.astype(BF16).astype(F32), (charge * pushed[1:2, :]).astype(BF16).astype(F32)]
    row_iota = lax.broadcasted_iota(jnp.int32, (64, 2048), 0)
    here = row_iota == row
    for c in range(2):
        row_hot[64 * c : 64 * (c + 1), :] = jnp.where(here, weights[c], 0.0).astype(BF16)
    place_iota = lax.broadcasted_iota(jnp.int32, (64, 2048), 0)

    def deposit_rows(step, carry):
        at = pl.multiple_of(step * 64, 64)
        hot = jnp.where(place_iota == place - at, 1.0, 0.0).astype(BF16)
        column_hot[pl.ds(at, 64), :] = hot
        rows = dot_nt(hot, row_hot[...]).astype(BF16)
        d_send[2 * step] = rows[:32]
        d_send[2 * step + 1] = rows[32:]
        return carry

    lax.fori_loop(0, 8, deposit_rows, 0)

    d_copies = []
    for k in range(1, 16):
        to = lax.rem(plane + k, 16)
        copy = pltpu.make_async_remote_copy(
            src_ref=d_send.at[to], dst_ref=d_recv.at[k - 1], send_sem=d_ssem.at[k - 1],
            recv_sem=d_rsem.at[k - 1], device_id=plane_peers[k - 1], device_id_type=MESH,
        )
        copy.start()
        d_copies.append(copy)

    for copy in a_copies:
        copy.wait_recv()
    part = a_send[plane]
    for k in range(15):
        part = part + a_recv[k]
    p_high, p_low = split(part.reshape(32, 128))
    twice = dot_nt(jnp.concatenate([p_high, p_low], axis=0), z_high[...])
    terms = twice[:32] + twice[32:] + dot_nt(p_high, z_low[...])
    for to in range(8):
        core_send[to % 2, to // 2] = terms[:, 128 * to : 128 * (to + 1)]
    core_copy = pltpu.make_async_remote_copy(
        src_ref=core_send.at[1 - core], dst_ref=core_recv, send_sem=c_ssem, recv_sem=c_rsem,
        device_id=sibling, device_id_type=MESH,
    )
    core_copy.start()
    core_copy.wait_recv()
    ring_send[...] = (core_send[core] + core_recv[...]).astype(BF16)

    r_copies = []
    for k in range(1, 16):
        copy = pltpu.make_async_remote_copy(
            src_ref=ring_send.at[ring_at[k - 1] // 4], dst_ref=ring_recv.at[k - 1],
            send_sem=r_ssem.at[k - 1], recv_sem=r_rsem.at[k - 1], device_id=ring_peers[k - 1],
            device_id_type=MESH,
        )
        copy.start()
        r_copies.append(copy)

    for copy in d_copies:
        copy.wait_recv()
    part = d_send[plane].astype(F32)
    for k in range(15):
        part = part + d_recv[k].astype(F32)
    e_send[...] = part.reshape(4, 8, 128)
    e_copies = []
    for k in range(1, 4):
        copy = pltpu.make_async_remote_copy(
            src_ref=e_send.at[low_at[k - 1]], dst_ref=e_recv.at[k - 1], send_sem=e_ssem.at[k - 1],
            recv_sem=e_rsem.at[k - 1], device_id=low_peers[k - 1], device_id_type=MESH,
        )
        copy.start()
        e_copies.append(copy)

    for copy in r_copies:
        copy.wait_recv()
    total = core_send[core, z_high_at] + core_recv[z_high_at]
    for k in range(15):
        total = total + ring_recv[k].astype(F32)
    slab_t[plane] = total.astype(BF16)
    g_copies = []
    for k in range(1, 16):
        copy = pltpu.make_async_remote_copy(
            src_ref=slab_t.at[plane], dst_ref=slab_t.at[plane], send_sem=g_ssem.at[k - 1],
            recv_sem=g_rsem.at[k - 1], device_id=plane_peers[k - 1], device_id_type=MESH,
        )
        copy.start()
        g_copies.append(copy)

    own = jnp.where(z_low_at == 0, total[0:8], 0.0)
    for zc in range(1, 4):
        own = own + jnp.where(z_low_at == zc, total[8 * zc : 8 * (zc + 1)], 0.0)
    field_ref[...] = own.T.reshape(2, 64, 8)
    for copy in e_copies:
        copy.wait_recv()
    own = e_send[z_low_at] + e_recv[0] + e_recv[1] + e_recv[2]
    deposit_ref[...] = own.T.reshape(2, 64, 8)
    kicked_ref[...] = pushed[...]

    for copy in g_copies:
        copy.wait_recv()
    sampled = dot_tn(slab_t[...].reshape(512, 128), column_hot[...])
    longitudinal = jnp.sum(jnp.where(here, sampled[:64], 0.0), axis=0, keepdims=True)
    transverse = jnp.sum(jnp.where(here, sampled[64:], 0.0), axis=0, keepdims=True)
    kicked_ref[5:6, :] = pushed[5:6, :] + 0.5 * longitudinal
    kicked_ref[1:2, :] = pushed[1:2, :] + 0.5 * transverse

    for copy in a_copies + d_copies + e_copies + [core_copy] + r_copies + g_copies:
        copy.wait_send()


def local(
    coords, charge, row_index, block_col, col_offset, transfer_map, history, retard_index, retard_frac,
    retard_weight, z_kernel, x_kernel,
):
    vmem = pl.BlockSpec(memory_space=pltpu.VMEM)
    smem = pl.BlockSpec(memory_space=pltpu.SMEM)
    anywhere = pl.BlockSpec(memory_space=pl.ANY)
    sem = pltpu.SemaphoreType.DMA
    return pl.pallas_call(
        kernel,
        out_shape=(
            jax.ShapeDtypeStruct((6, 2048), F32),
            jax.ShapeDtypeStruct((2, 64, 8), F32),
            jax.ShapeDtypeStruct((2, 64, 8), F32),
        ),
        in_specs=[
            vmem, vmem, vmem, smem, vmem, vmem, anywhere, smem, smem, smem, anywhere, anywhere,
        ],
        out_specs=(vmem, vmem, vmem),
        scratch_shapes=[
            pltpu.VMEM((8, 2, 64, 512), BF16),
            pltpu.VMEM((512, 512), F32),
            pltpu.VMEM((512, 64), F32),
            pltpu.VMEM((128, 512), F32),
            pltpu.VMEM((8, 128), F32),
            pltpu.VMEM((512, 512), BF16),
            pltpu.VMEM((512, 512), BF16),
            pltpu.VMEM((1024, 128), BF16),
            pltpu.VMEM((1024, 128), BF16),
            pltpu.VMEM((16, 4, 8, 128), F32),
            pltpu.VMEM((15, 4, 8, 128), F32),
            pltpu.VMEM((16, 32, 128), BF16),
            pltpu.VMEM((15, 32, 128), BF16),
            pltpu.VMEM((4, 8, 128), F32),
            pltpu.VMEM((3, 8, 128), F32),
            pltpu.VMEM((2, 4, 32, 128), F32),
            pltpu.VMEM((4, 32, 128), F32),
            pltpu.VMEM((4, 32, 128), BF16),
            pltpu.VMEM((15, 32, 128), BF16),
            pltpu.VMEM((16, 32, 128), BF16),
            pltpu.VMEM((512, 2048), BF16),
            pltpu.VMEM((128, 2048), BF16),
            pltpu.VMEM((6, 2048), F32),
            sem((3,)),
            sem((15,)), sem((15,)),
            sem((15,)), sem((15,)),
            sem((3,)), sem((3,)),
            sem, sem,
            sem((15,)), sem((15,)),
            sem((15,)), sem((15,)),
        ],
        compiler_params=pltpu.CompilerParams(
            collective_id=0, has_side_effects=True, vmem_limit_bytes=40 * 1024 * 1024
        ),
        cost_estimate=pl.CostEstimate(flops=10**9, bytes_accessed=4 * 10**6, transcendentals=0),
    )(
        coords,
        charge.reshape(1, -1),
        row_index.reshape(1, -1),
        block_col,
        col_offset.reshape(1, -1),
        transfer_map,
        history,
        retard_index,
        retard_frac,
        retard_weight,
        z_kernel,
        x_kernel,
    )


def solution(mesh):
    return jax.shard_map(
        local,
        mesh=mesh,
        in_specs=(
            P(None, ("dom", "hist")),
            P(("dom", "hist")),
            P(("dom", "hist")),
            P(("dom", "hist")),
            P(("dom", "hist")),
            P(),
            P("hist", None, "dom", None),
            P("hist"),
            P("hist"),
            P("hist"),
            P(None, "dom"),
            P(),
        ),
        out_specs=(P(None, ("dom", "hist")), P(None, "dom", "hist"), P(None, "dom", "hist")),
        check_vma=False,
    )
```

```python
import jax
import jax.numpy as jnp
from jax import lax
from jax.experimental import pallas as pl
from jax.experimental.pallas import tpu as pltpu
from jax.sharding import PartitionSpec as P

MESH = pl.DeviceIdType.MESH
F32 = jnp.float32
BF16 = jnp.bfloat16


def split(value):
    high = value.astype(BF16)
    return high, (value - high.astype(F32)).astype(BF16)


def dot_nn(a, b):
    return lax.dot_general(a, b, (((1,), (0,)), ((), ())), preferred_element_type=F32)


def dot_nt(a, b):
    return lax.dot_general(a, b, (((1,), (1,)), ((), ())), preferred_element_type=F32)


def dot_tn(a, b):
    return lax.dot_general(a, b, (((0,), (0,)), ((), ())), preferred_element_type=F32)


def kernel(
    coords_hbm, charge_hbm, row_hbm, block_hbm, offset_hbm, map_hbm, history_hbm, lag_hbm, frac_hbm,
    weight_hbm, z_hbm, x_hbm,
    kicked_ref, field_ref, deposit_ref,
    coords_ref, charge_ref, row_ref, block_ref, offset_ref, map_ref, lag_ref, frac_ref, weight_ref,
    history, x_full, z_own, near, x_high, x_low, z_high, z_low,
    a_send, a_recv, d_send, d_recv, e_send, e_recv, core_send, core_recv, ring_send, ring_recv,
    slab_t, column_hot, row_hot, pushed,
    load_sem, a_ssem, a_rsem, d_ssem, d_rsem, e_ssem, e_rsem, c_ssem, c_rsem, r_ssem, r_rsem,
    g_ssem, g_rsem, far_sem,
):
    hist = lax.axis_index("hist")
    dom = lax.axis_index("dom")
    z_low_at, plane = hist // 16, hist % 16
    z_high_at, core = dom // 2, dom % 2
    z_at = z_high_at * 4 + z_low_at

    plane_steps = sorted(
        [(a, b) for a in range(4) for b in range(4) if a or b],
        key=lambda step: -(min(step[0], 4 - step[0]) + min(step[1], 4 - step[1])),
    )
    plane_at = [lax.rem(plane // 4 + a, 4) * 4 + lax.rem(plane % 4 + b, 4) for a, b in plane_steps]
    plane_peers = [{"hist": z_low_at * 16 + at, "dom": dom} for at in plane_at]
    ring_steps = sorted(range(1, 16), key=lambda k: -min(k, 16 - k))
    ring_at = [lax.rem(z_at + k, 16) for k in ring_steps]
    ring_peers = [{"hist": (at % 4) * 16 + plane, "dom": (at // 4) * 2 + core} for at in ring_at]
    ring_near = [peer for k, peer in zip(ring_steps, ring_peers) if min(k, 16 - k) <= 4]
    ring_four = [peer for k, peer in zip(ring_steps, ring_peers) if min(k, 16 - k) == 4]
    low_at = [lax.rem(z_low_at + k, 4) for k in range(1, 4)]
    low_peers = [{"hist": at * 16 + plane, "dom": dom} for at in low_at]
    sibling = {"hist": hist, "dom": z_high_at * 2 + (1 - core)}

    def load(index, source, target):
        copy = pltpu.make_async_copy(source, target, load_sem.at[index])
        copy.start()
        return copy

    load_history = load(0, history_hbm, history)
    load_steps = [load(1, lag_hbm, lag_ref), load(2, frac_hbm, frac_ref), load(3, weight_hbm, weight_ref)]
    load_x = load(4, x_hbm, x_full)
    barrier = pltpu.get_barrier_semaphore()
    for peer in plane_peers + ring_near + [sibling]:
        pl.semaphore_signal(barrier, inc=1, device_id=peer, device_id_type=MESH)

    load_z = load(5, z_hbm, z_own)
    load_particles = [
        load(6, coords_hbm, coords_ref), load(7, charge_hbm, charge_ref), load(8, row_hbm, row_ref),
        load(9, block_hbm, block_ref), load(10, offset_hbm, offset_ref), load(11, map_hbm, map_ref),
    ]

    lane = lax.broadcasted_iota(jnp.int32, (32, 128), 1)
    for copy in load_steps:
        copy.wait()
    load_history.wait()

    def source_rows(group, carry):
        comp = group // 2
        row = pl.multiple_of((group % 2) * 32, 32)
        row_out = pl.multiple_of(group * 32, 32)
        near_sum = [jnp.zeros((32, 128), F32) for _ in range(4)]
        far_sum = [jnp.zeros((32, 128), F32) for _ in range(4)]
        for t in range(8):
            lag = lag_ref[t]
            fraction = frac_ref[t]
            weight = weight_ref[t]
            near_weight = weight * (1.0 - fraction)
            far_weight = weight * fraction
            inside = lane >= lag
            before = jnp.zeros((32, 128), F32)
            for j in range(4):
                piece = history[t, comp, pl.ds(row, 32), 128 * j : 128 * (j + 1)].astype(F32)
                turned = pltpu.roll(piece, lag, 1)
                moved = jnp.where(inside, turned, before)
                before = turned
                near_sum[j] = near_sum[j] + near_weight * moved
                far_sum[j] = far_sum[j] + far_weight * moved
        before = jnp.zeros((32, 128), F32)
        for j in range(4):
            turned = pltpu.roll(far_sum[j], 1, 1)
            near[pl.ds(row_out, 32), 128 * j : 128 * (j + 1)] = near_sum[j] + jnp.where(
                lane >= 1, turned, before
            )
            before = turned
        return carry

    lax.fori_loop(0, 4, source_rows, 0)

    load_x.wait()
    x_high[...], x_low[...] = split(x_full[...])
    s_high, s_low = split(near[...])
    twice = dot_nn(jnp.concatenate([s_high, s_low], axis=0), x_high[...])
    spread = twice[:128] + twice[128:] + dot_nn(s_high, x_low[...])
    spread_t = spread.T.reshape(4, 16, 8, 128)
    for zc in range(4):
        a_send[:, zc] = spread_t[zc]

    pl.semaphore_wait(barrier, 24)
    for peer in ring_four:
        pl.semaphore_signal(far_sem, inc=1, device_id=peer, device_id_type=MESH)

    a_copies = []
    for k in range(1, 16):
        to = plane_at[k - 1]
        copy = pltpu.make_async_remote_copy(
            src_ref=a_send.at[to], dst_ref=a_recv.at[k - 1], send_sem=a_ssem.at[k - 1],
            recv_sem=a_rsem.at[k - 1], device_id=plane_peers[k - 1], device_id_type=MESH,
        )
        copy.start()
        a_copies.append(copy)

    load_z.wait()
    empty = jnp.zeros((64, 64), F32)
    for to in range(8):
        block = z_own[:, 64 * to : 64 * (to + 1)]
        pair = jnp.concatenate(
            [jnp.concatenate([block, empty], axis=1), jnp.concatenate([empty, block], axis=1)], axis=0
        )
        z_high[:, 128 * to : 128 * (to + 1)], z_low[:, 128 * to : 128 * (to + 1)] = split(pair)

    for copy in load_particles:
        copy.wait()
    for chunk in range(4):
        lanes = slice(512 * chunk, 512 * (chunk + 1))
        wide = [jnp.broadcast_to(coords_ref[i : i + 1, lanes], (6, 512)) for i in range(6)]
        total = jnp.broadcast_to(map_ref[:, 0:1], (6, 512))
        at = 1
        for i in range(6):
            total = total + map_ref[:, at : at + 1] * wide[i]
            at += 1
        for i in range(6):
            for j in range(i, 6):
                total = total + map_ref[:, at : at + 1] * (wide[i] * wide[j])
                at += 1
        for i in range(6):
            for j in range(i, 6):
                two = wide[i] * wide[j]
                for k in range(j, 6):
                    total = total + map_ref[:, at : at + 1] * (two * wide[k])
                    at += 1
        pushed[:, lanes] = total

    row = row_ref[...] - dom * 64
    first = jnp.concatenate([jnp.full((1, 128), block_ref[b], jnp.int32) for b in range(16)], axis=1)
    column = first + offset_ref[...]
    place = ((column >> 3) & 15) * 32 + (column >> 7) * 8 + (column & 7)
    charge = charge_ref[...]
    weights = [charge.astype(BF16).astype(F32), (charge * pushed[1:2, :]).astype(BF16).astype(F32)]
    row_iota = lax.broadcasted_iota(jnp.int32, (64, 2048), 0)
    here = row_iota == row
    for c in range(2):
        row_hot[64 * c : 64 * (c + 1), :] = jnp.where(here, weights[c], 0.0).astype(BF16)
    place_iota = lax.broadcasted_iota(jnp.int32, (64, 2048), 0)

    def deposit_rows(step, carry):
        at = pl.multiple_of(step * 64, 64)
        hot = jnp.where(place_iota == place - at, 1.0, 0.0).astype(BF16)
        column_hot[pl.ds(at, 64), :] = hot
        rows = dot_nt(hot, row_hot[...]).astype(BF16)
        d_send[2 * step] = rows[:32]
        d_send[2 * step + 1] = rows[32:]
        return carry

    lax.fori_loop(0, 8, deposit_rows, 0)

    d_copies = []
    for k in range(1, 16):
        to = plane_at[k - 1]
        copy = pltpu.make_async_remote_copy(
            src_ref=d_send.at[to], dst_ref=d_recv.at[k - 1], send_sem=d_ssem.at[k - 1],
            recv_sem=d_rsem.at[k - 1], device_id=plane_peers[k - 1], device_id_type=MESH,
        )
        copy.start()
        d_copies.append(copy)

    for copy in a_copies:
        copy.wait_recv()
    part = a_send[plane]
    for k in range(15):
        part = part + a_recv[k]
    p_high, p_low = split(part.reshape(32, 128))
    twice = dot_nn(jnp.concatenate([p_high, p_low], axis=0), z_high[...])
    terms = twice[:32] + twice[32:] + dot_nn(p_high, z_low[...])
    for to in range(8):
        core_send[to % 2, to // 2] = terms[:, 128 * to : 128 * (to + 1)]
    core_copy = pltpu.make_async_remote_copy(
        src_ref=core_send.at[1 - core], dst_ref=core_recv, send_sem=c_ssem, recv_sem=c_rsem,
        device_id=sibling, device_id_type=MESH,
    )
    core_copy.start()
    core_copy.wait_recv()
    ring_send[...] = (core_send[core] + core_recv[...]).astype(BF16)

    pl.semaphore_wait(far_sem, 2)
    r_copies = []
    for k in range(1, 16):
        copy = pltpu.make_async_remote_copy(
            src_ref=ring_send.at[ring_at[k - 1] // 4], dst_ref=ring_recv.at[k - 1],
            send_sem=r_ssem.at[k - 1], recv_sem=r_rsem.at[k - 1], device_id=ring_peers[k - 1],
            device_id_type=MESH,
        )
        copy.start()
        r_copies.append(copy)

    for copy in d_copies:
        copy.wait_recv()
    part = d_send[plane].astype(F32)
    for k in range(15):
        part = part + d_recv[k].astype(F32)
    e_send[...] = part.reshape(4, 8, 128)
    e_copies = []
    for k in range(1, 4):
        copy = pltpu.make_async_remote_copy(
            src_ref=e_send.at[low_at[k - 1]], dst_ref=e_recv.at[k - 1], send_sem=e_ssem.at[k - 1],
            recv_sem=e_rsem.at[k - 1], device_id=low_peers[k - 1], device_id_type=MESH,
        )
        copy.start()
        e_copies.append(copy)

    for copy in r_copies:
        copy.wait_recv()
    total = core_send[core, z_high_at] + core_recv[z_high_at]
    for k in range(15):
        total = total + ring_recv[k].astype(F32)
    slab_t[plane] = total.astype(BF16)
    g_copies = []
    for k in range(1, 16):
        copy = pltpu.make_async_remote_copy(
            src_ref=slab_t.at[plane], dst_ref=slab_t.at[plane], send_sem=g_ssem.at[k - 1],
            recv_sem=g_rsem.at[k - 1], device_id=plane_peers[k - 1], device_id_type=MESH,
        )
        copy.start()
        g_copies.append(copy)

    own = jnp.where(z_low_at == 0, total[0:8], 0.0)
    for zc in range(1, 4):
        own = own + jnp.where(z_low_at == zc, total[8 * zc : 8 * (zc + 1)], 0.0)
    field_ref[0] = own[:, :64]
    field_ref[1] = own[:, 64:]
    for copy in e_copies:
        copy.wait_recv()
    own = e_send[z_low_at] + e_recv[0] + e_recv[1] + e_recv[2]
    deposit_ref[0] = own[:, :64]
    deposit_ref[1] = own[:, 64:]
    kicked_ref[...] = pushed[...]

    for copy in g_copies:
        copy.wait_recv()
    sampled = dot_tn(slab_t[...].reshape(512, 128), column_hot[...])
    longitudinal = jnp.sum(jnp.where(here, sampled[:64], 0.0), axis=0, keepdims=True)
    transverse = jnp.sum(jnp.where(here, sampled[64:], 0.0), axis=0, keepdims=True)
    kicked_ref[5:6, :] = pushed[5:6, :] + 0.5 * longitudinal
    kicked_ref[1:2, :] = pushed[1:2, :] + 0.5 * transverse

    for copy in a_copies + d_copies + e_copies + [core_copy] + r_copies + g_copies:
        copy.wait_send()


def place(kicked_in, field_in, deposit_in, kicked_ref, field_ref, deposit_ref, sems):
    copies = [
        pltpu.make_async_copy(kicked_in, kicked_ref, sems.at[0]),
        pltpu.make_async_copy(field_in, field_ref, sems.at[1]),
        pltpu.make_async_copy(deposit_in, deposit_ref, sems.at[2]),
    ]
    for copy in copies:
        copy.start()
    for copy in copies:
        copy.wait()


def local(
    coords, charge, row_index, block_col, col_offset, transfer_map, history, retard_index, retard_frac,
    retard_weight, z_kernel, x_kernel,
):
    vmem = pl.BlockSpec(memory_space=pltpu.VMEM)
    hbm = pl.BlockSpec(memory_space=pltpu.HBM)
    sem = pltpu.SemaphoreType.DMA
    shapes = (
        jax.ShapeDtypeStruct((6, 2048), F32),
        jax.ShapeDtypeStruct((2, 8, 64), F32),
        jax.ShapeDtypeStruct((2, 8, 64), F32),
    )
    results = pl.pallas_call(
        kernel,
        out_shape=tuple(pltpu.VMEM(shape.shape, shape.dtype) for shape in shapes),
        in_specs=[hbm] * 12,
        out_specs=(vmem, vmem, vmem),
        scratch_shapes=[
            pltpu.VMEM((6, 2048), F32),
            pltpu.VMEM((1, 2048), F32),
            pltpu.VMEM((1, 2048), jnp.int32),
            pltpu.SMEM((16,), jnp.int32),
            pltpu.VMEM((1, 2048), jnp.int32),
            pltpu.VMEM((6, 84), F32),
            pltpu.SMEM((8,), jnp.int32),
            pltpu.SMEM((8,), F32),
            pltpu.SMEM((8,), F32),
            pltpu.VMEM((8, 2, 64, 512), BF16),
            pltpu.VMEM((512, 512), F32),
            pltpu.VMEM((64, 512), F32),
            pltpu.VMEM((128, 512), F32),
            pltpu.VMEM((512, 512), BF16),
            pltpu.VMEM((512, 512), BF16),
            pltpu.VMEM((128, 1024), BF16),
            pltpu.VMEM((128, 1024), BF16),
            pltpu.VMEM((16, 4, 8, 128), F32),
            pltpu.VMEM((15, 4, 8, 128), F32),
            pltpu.VMEM((16, 32, 128), BF16),
            pltpu.VMEM((15, 32, 128), BF16),
            pltpu.VMEM((4, 8, 128), F32),
            pltpu.VMEM((3, 8, 128), F32),
            pltpu.VMEM((2, 4, 32, 128), F32),
            pltpu.VMEM((4, 32, 128), F32),
            pltpu.VMEM((4, 32, 128), BF16),
            pltpu.VMEM((15, 32, 128), BF16),
            pltpu.VMEM((16, 32, 128), BF16),
            pltpu.VMEM((512, 2048), BF16),
            pltpu.VMEM((128, 2048), BF16),
            pltpu.VMEM((6, 2048), F32),
            sem((12,)),
            sem((15,)), sem((15,)),
            sem((15,)), sem((15,)),
            sem((3,)), sem((3,)),
            sem, sem,
            sem((15,)), sem((15,)),
            sem((15,)), sem((15,)), pltpu.SemaphoreType.REGULAR,
        ],
        compiler_params=pltpu.CompilerParams(
            collective_id=0, has_side_effects=True, vmem_limit_bytes=58 * 1024 * 1024
        ),
        cost_estimate=pl.CostEstimate(flops=10**9, bytes_accessed=4 * 10**6, transcendentals=0),
    )(
        coords,
        charge.reshape(1, -1),
        row_index.reshape(1, -1),
        block_col,
        col_offset.reshape(1, -1),
        transfer_map,
        history,
        retard_index,
        retard_frac,
        retard_weight,
        z_kernel.T,
        x_kernel,
    )
    anywhere = pl.BlockSpec(memory_space=pl.ANY)
    kicked, field, deposit = pl.pallas_call(
        place,
        out_shape=shapes,
        in_specs=[vmem] * 3,
        out_specs=(anywhere,) * 3,
        scratch_shapes=[sem((3,))],
        cost_estimate=pl.CostEstimate(flops=0, bytes_accessed=10**5, transcendentals=0),
    )(*[pltpu.with_memory_space_constraint(r, pltpu.VMEM) for r in results])
    return kicked, jnp.swapaxes(field, 1, 2), jnp.swapaxes(deposit, 1, 2)


def solution(mesh):
    return jax.shard_map(
        local,
        mesh=mesh,
        in_specs=(
            P(None, ("dom", "hist")),
            P(("dom", "hist")),
            P(("dom", "hist")),
            P(("dom", "hist")),
            P(("dom", "hist")),
            P(),
            P("hist", None, "dom", None),
            P("hist"),
            P("hist"),
            P("hist"),
            P(None, "dom"),
            P(),
        ),
        out_specs=(P(None, ("dom", "hist")), P(None, "dom", "hist"), P(None, "dom", "hist")),
        check_vma=False,
    )
```

```python
import jax
import jax.numpy as jnp
from jax import lax
from jax.experimental import pallas as pl
from jax.experimental.pallas import tpu as pltpu
from jax.sharding import PartitionSpec as P

MESH = pl.DeviceIdType.MESH
F32 = jnp.float32
BF16 = jnp.bfloat16


def split(value):
    high = value.astype(BF16)
    return high, (value - high.astype(F32)).astype(BF16)


def dot_nn(a, b):
    return lax.dot_general(a, b, (((1,), (0,)), ((), ())), preferred_element_type=F32)


def dot_nt(a, b):
    return lax.dot_general(a, b, (((1,), (1,)), ((), ())), preferred_element_type=F32)


def dot_tn(a, b):
    return lax.dot_general(a, b, (((0,), (0,)), ((), ())), preferred_element_type=F32)


def kernel(
    coords_hbm, charge_hbm, row_hbm, block_hbm, offset_hbm, map_hbm, history_hbm, lag_hbm, frac_hbm,
    weight_hbm, z_hbm, x_hbm,
    kicked_ref, field_ref, deposit_ref,
    coords_ref, charge_ref, row_ref, block_ref, offset_ref, map_ref, lag_ref, frac_ref, weight_ref,
    history, x_full, z_own, near, x_high, x_low, z_high, z_low,
    a_send, a_recv, d_send, d_recv, e_send, e_recv, core_send, core_recv, ring_send, ring_recv,
    slab_t, column_hot, row_hot, pushed,
    load_sem, a_ssem, a_rsem, d_ssem, d_rsem, e_ssem, e_rsem, c_ssem, c_rsem, r_ssem, r_rsem,
    g_ssem, g_rsem, far_sem,
):
    hist = lax.axis_index("hist")
    dom = lax.axis_index("dom")
    z_low_at, plane = hist // 16, hist % 16
    z_high_at, core = dom // 2, dom % 2
    z_at = z_high_at * 4 + z_low_at

    plane_steps = sorted(
        [(a, b) for a in range(4) for b in range(4) if a or b],
        key=lambda step: -(min(step[0], 4 - step[0]) + min(step[1], 4 - step[1])),
    )
    plane_at = [lax.rem(plane // 4 + a, 4) * 4 + lax.rem(plane % 4 + b, 4) for a, b in plane_steps]
    plane_peers = [{"hist": z_low_at * 16 + at, "dom": dom} for at in plane_at]
    ring_steps = sorted(range(1, 16), key=lambda k: -min(k, 16 - k))
    ring_at = [lax.rem(z_at + k, 16) for k in ring_steps]
    ring_peers = [{"hist": (at % 4) * 16 + plane, "dom": (at // 4) * 2 + core} for at in ring_at]
    ring_near = [peer for k, peer in zip(ring_steps, ring_peers) if min(k, 16 - k) <= 4]
    ring_four = [peer for k, peer in zip(ring_steps, ring_peers) if min(k, 16 - k) == 4]
    low_at = [lax.rem(z_low_at + k, 4) for k in range(1, 4)]
    low_peers = [{"hist": at * 16 + plane, "dom": dom} for at in low_at]
    def stage(buffer, send_sem, recv_sem):
        return pltpu.make_async_remote_copy(
            src_ref=buffer, dst_ref=buffer, send_sem=send_sem, recv_sem=recv_sem,
            device_id=plane_peers[0], device_id_type=MESH,
        )

    a_stage = stage(a_recv, a_ssem, a_rsem)
    d_stage = stage(d_recv, d_ssem, d_rsem)
    e_stage = stage(e_recv, e_ssem, e_rsem)
    r_stage = stage(ring_recv, r_ssem, r_rsem)
    g_stage = stage(slab_t.at[0:15], g_ssem, g_rsem)
    sibling = {"hist": hist, "dom": z_high_at * 2 + (1 - core)}

    def load(index, source, target):
        copy = pltpu.make_async_copy(source, target, load_sem.at[index])
        copy.start()
        return copy

    load_history = load(0, history_hbm, history)
    load_steps = [load(1, lag_hbm, lag_ref), load(2, frac_hbm, frac_ref), load(3, weight_hbm, weight_ref)]
    load_x = load(4, x_hbm, x_full)
    barrier = pltpu.get_barrier_semaphore()
    for peer in plane_peers + ring_near + [sibling]:
        pl.semaphore_signal(barrier, inc=1, device_id=peer, device_id_type=MESH)

    load_z = load(5, z_hbm, z_own)
    load_particles = [
        load(6, coords_hbm, coords_ref), load(7, charge_hbm, charge_ref), load(8, row_hbm, row_ref),
        load(9, block_hbm, block_ref), load(10, offset_hbm, offset_ref), load(11, map_hbm, map_ref),
    ]

    lane = lax.broadcasted_iota(jnp.int32, (32, 128), 1)
    for copy in load_steps:
        copy.wait()
    load_history.wait()

    def source_rows(group, carry):
        comp = group // 2
        row = pl.multiple_of((group % 2) * 32, 32)
        row_out = pl.multiple_of(group * 32, 32)
        near_sum = [jnp.zeros((32, 128), F32) for _ in range(4)]
        far_sum = [jnp.zeros((32, 128), F32) for _ in range(4)]
        for t in range(8):
            lag = lag_ref[t]
            fraction = frac_ref[t]
            weight = weight_ref[t]
            near_weight = weight * (1.0 - fraction)
            far_weight = weight * fraction
            inside = lane >= lag
            before = jnp.zeros((32, 128), F32)
            for j in range(4):
                piece = history[t, comp, pl.ds(row, 32), 128 * j : 128 * (j + 1)].astype(F32)
                turned = pltpu.roll(piece, lag, 1)
                moved = jnp.where(inside, turned, before)
                before = turned
                near_sum[j] = near_sum[j] + near_weight * moved
                far_sum[j] = far_sum[j] + far_weight * moved
        before = jnp.zeros((32, 128), F32)
        for j in range(4):
            turned = pltpu.roll(far_sum[j], 1, 1)
            near[pl.ds(row_out, 32), 128 * j : 128 * (j + 1)] = near_sum[j] + jnp.where(
                lane >= 1, turned, before
            )
            before = turned
        return carry

    lax.fori_loop(0, 4, source_rows, 0)

    load_x.wait()
    x_high[...], x_low[...] = split(x_full[...])
    s_high, s_low = split(near[...])
    twice = dot_nn(jnp.concatenate([s_high, s_low], axis=0), x_high[...])
    spread = twice[:128] + twice[128:] + dot_nn(s_high, x_low[...])
    spread_t = spread.T.reshape(4, 16, 8, 128)
    for zc in range(4):
        a_send[:, zc] = spread_t[zc]

    pl.semaphore_wait(barrier, 24)
    for peer in ring_four:
        pl.semaphore_signal(far_sem, inc=1, device_id=peer, device_id_type=MESH)

    for k in range(1, 16):
        to = plane_at[k - 1]
        copy = pltpu.make_async_remote_copy(
            src_ref=a_send.at[to], dst_ref=a_recv.at[k - 1], send_sem=a_ssem,
            recv_sem=a_rsem, device_id=plane_peers[k - 1], device_id_type=MESH,
        )
        copy.start()

    load_z.wait()
    empty = jnp.zeros((64, 64), F32)
    for to in range(8):
        block = z_own[:, 64 * to : 64 * (to + 1)]
        pair = jnp.concatenate(
            [jnp.concatenate([block, empty], axis=1), jnp.concatenate([empty, block], axis=1)], axis=0
        )
        z_high[:, 128 * to : 128 * (to + 1)], z_low[:, 128 * to : 128 * (to + 1)] = split(pair)

    for copy in load_particles:
        copy.wait()
    for chunk in range(4):
        lanes = slice(512 * chunk, 512 * (chunk + 1))
        wide = [jnp.broadcast_to(coords_ref[i : i + 1, lanes], (6, 512)) for i in range(6)]
        total = jnp.broadcast_to(map_ref[:, 0:1], (6, 512))
        at = 1
        for i in range(6):
            total = total + map_ref[:, at : at + 1] * wide[i]
            at += 1
        for i in range(6):
            for j in range(i, 6):
                total = total + map_ref[:, at : at + 1] * (wide[i] * wide[j])
                at += 1
        for i in range(6):
            for j in range(i, 6):
                two = wide[i] * wide[j]
                for k in range(j, 6):
                    total = total + map_ref[:, at : at + 1] * (two * wide[k])
                    at += 1
        pushed[:, lanes] = total

    row = row_ref[...] - dom * 64
    first = jnp.concatenate([jnp.full((1, 128), block_ref[b], jnp.int32) for b in range(16)], axis=1)
    column = first + offset_ref[...]
    place = ((column >> 3) & 15) * 32 + (column >> 7) * 8 + (column & 7)
    charge = charge_ref[...]
    weights = [charge.astype(BF16).astype(F32), (charge * pushed[1:2, :]).astype(BF16).astype(F32)]
    row_iota = lax.broadcasted_iota(jnp.int32, (64, 2048), 0)
    here = row_iota == row
    for c in range(2):
        row_hot[64 * c : 64 * (c + 1), :] = jnp.where(here, weights[c], 0.0).astype(BF16)
    place_iota = lax.broadcasted_iota(jnp.int32, (64, 2048), 0)

    def deposit_rows(step, carry):
        at = pl.multiple_of(step * 64, 64)
        hot = jnp.where(place_iota == place - at, 1.0, 0.0).astype(BF16)
        column_hot[pl.ds(at, 64), :] = hot
        rows = dot_nt(hot, row_hot[...]).astype(BF16)
        d_send[2 * step] = rows[:32]
        d_send[2 * step + 1] = rows[32:]
        return carry

    lax.fori_loop(0, 8, deposit_rows, 0)

    for k in range(1, 16):
        to = plane_at[k - 1]
        copy = pltpu.make_async_remote_copy(
            src_ref=d_send.at[to], dst_ref=d_recv.at[k - 1], send_sem=d_ssem,
            recv_sem=d_rsem, device_id=plane_peers[k - 1], device_id_type=MESH,
        )
        copy.start()

    a_stage.wait_recv()
    part = a_send[plane]
    for k in range(15):
        part = part + a_recv[k]
    p_high, p_low = split(part.reshape(32, 128))
    twice = dot_nn(jnp.concatenate([p_high, p_low], axis=0), z_high[...])
    terms = twice[:32] + twice[32:] + dot_nn(p_high, z_low[...])
    for to in range(8):
        core_send[to % 2, to // 2] = terms[:, 128 * to : 128 * (to + 1)]
    core_copy = pltpu.make_async_remote_copy(
        src_ref=core_send.at[1 - core], dst_ref=core_recv, send_sem=c_ssem, recv_sem=c_rsem,
        device_id=sibling, device_id_type=MESH,
    )
    core_copy.start()
    core_copy.wait_recv()
    ring_send[...] = (core_send[core] + core_recv[...]).astype(BF16)

    pl.semaphore_wait(far_sem, 2)
    for k in range(1, 16):
        copy = pltpu.make_async_remote_copy(
            src_ref=ring_send.at[ring_at[k - 1] // 4], dst_ref=ring_recv.at[k - 1],
            send_sem=r_ssem, recv_sem=r_rsem, device_id=ring_peers[k - 1],
            device_id_type=MESH,
        )
        copy.start()

    d_stage.wait_recv()
    part = d_send[plane].astype(F32)
    for k in range(15):
        part = part + d_recv[k].astype(F32)
    e_send[...] = part.reshape(4, 8, 128)
    for k in range(1, 4):
        copy = pltpu.make_async_remote_copy(
            src_ref=e_send.at[low_at[k - 1]], dst_ref=e_recv.at[k - 1], send_sem=e_ssem,
            recv_sem=e_rsem, device_id=low_peers[k - 1], device_id_type=MESH,
        )
        copy.start()

    r_stage.wait_recv()
    total = core_send[core, z_high_at] + core_recv[z_high_at]
    for k in range(15):
        total = total + ring_recv[k].astype(F32)
    slab_t[plane] = total.astype(BF16)
    for k in range(1, 16):
        copy = pltpu.make_async_remote_copy(
            src_ref=slab_t.at[plane], dst_ref=slab_t.at[plane], send_sem=g_ssem,
            recv_sem=g_rsem, device_id=plane_peers[k - 1], device_id_type=MESH,
        )
        copy.start()

    own = jnp.where(z_low_at == 0, total[0:8], 0.0)
    for zc in range(1, 4):
        own = own + jnp.where(z_low_at == zc, total[8 * zc : 8 * (zc + 1)], 0.0)
    field_ref[0] = own[:, :64]
    field_ref[1] = own[:, 64:]
    e_stage.wait_recv()
    own = e_send[z_low_at] + e_recv[0] + e_recv[1] + e_recv[2]
    deposit_ref[0] = own[:, :64]
    deposit_ref[1] = own[:, 64:]
    kicked_ref[...] = pushed[...]

    for part in (a_stage, d_stage, e_stage, core_copy, r_stage):
        part.wait_send()

    g_stage.wait_recv()
    sampled = dot_tn(slab_t[...].reshape(512, 128), column_hot[...])
    longitudinal = jnp.sum(jnp.where(here, sampled[:64], 0.0), axis=0, keepdims=True)
    transverse = jnp.sum(jnp.where(here, sampled[64:], 0.0), axis=0, keepdims=True)
    kicked_ref[5:6, :] = pushed[5:6, :] + 0.5 * longitudinal
    kicked_ref[1:2, :] = pushed[1:2, :] + 0.5 * transverse

    g_stage.wait_send()


def place(kicked_in, field_in, deposit_in, kicked_ref, field_ref, deposit_ref, sems):
    copies = [
        pltpu.make_async_copy(kicked_in, kicked_ref, sems.at[0]),
        pltpu.make_async_copy(field_in, field_ref, sems.at[1]),
        pltpu.make_async_copy(deposit_in, deposit_ref, sems.at[2]),
    ]
    for copy in copies:
        copy.start()
    for copy in copies:
        copy.wait()


def local(
    coords, charge, row_index, block_col, col_offset, transfer_map, history, retard_index, retard_frac,
    retard_weight, z_kernel, x_kernel,
):
    vmem = pl.BlockSpec(memory_space=pltpu.VMEM)
    hbm = pl.BlockSpec(memory_space=pltpu.HBM)
    sem = pltpu.SemaphoreType.DMA
    shapes = (
        jax.ShapeDtypeStruct((6, 2048), F32),
        jax.ShapeDtypeStruct((2, 8, 64), F32),
        jax.ShapeDtypeStruct((2, 8, 64), F32),
    )
    results = pl.pallas_call(
        kernel,
        out_shape=tuple(pltpu.VMEM(shape.shape, shape.dtype) for shape in shapes),
        in_specs=[hbm] * 12,
        out_specs=(vmem, vmem, vmem),
        scratch_shapes=[
            pltpu.VMEM((6, 2048), F32),
            pltpu.VMEM((1, 2048), F32),
            pltpu.VMEM((1, 2048), jnp.int32),
            pltpu.SMEM((16,), jnp.int32),
            pltpu.VMEM((1, 2048), jnp.int32),
            pltpu.VMEM((6, 84), F32),
            pltpu.SMEM((8,), jnp.int32),
            pltpu.SMEM((8,), F32),
            pltpu.SMEM((8,), F32),
            pltpu.VMEM((8, 2, 64, 512), BF16),
            pltpu.VMEM((512, 512), F32),
            pltpu.VMEM((64, 512), F32),
            pltpu.VMEM((128, 512), F32),
            pltpu.VMEM((512, 512), BF16),
            pltpu.VMEM((512, 512), BF16),
            pltpu.VMEM((128, 1024), BF16),
            pltpu.VMEM((128, 1024), BF16),
            pltpu.VMEM((16, 4, 8, 128), F32),
            pltpu.VMEM((15, 4, 8, 128), F32),
            pltpu.VMEM((16, 32, 128), BF16),
            pltpu.VMEM((15, 32, 128), BF16),
            pltpu.VMEM((4, 8, 128), F32),
            pltpu.VMEM((3, 8, 128), F32),
            pltpu.VMEM((2, 4, 32, 128), F32),
            pltpu.VMEM((4, 32, 128), F32),
            pltpu.VMEM((4, 32, 128), BF16),
            pltpu.VMEM((15, 32, 128), BF16),
            pltpu.VMEM((16, 32, 128), BF16),
            pltpu.VMEM((512, 2048), BF16),
            pltpu.VMEM((128, 2048), BF16),
            pltpu.VMEM((6, 2048), F32),
            sem((12,)),
            sem, sem,
            sem, sem,
            sem, sem,
            sem, sem,
            sem, sem,
            sem, sem, pltpu.SemaphoreType.REGULAR,
        ],
        compiler_params=pltpu.CompilerParams(
            collective_id=0, has_side_effects=True, vmem_limit_bytes=58 * 1024 * 1024
        ),
        cost_estimate=pl.CostEstimate(flops=10**9, bytes_accessed=4 * 10**6, transcendentals=0),
    )(
        coords,
        charge.reshape(1, -1),
        row_index.reshape(1, -1),
        block_col,
        col_offset.reshape(1, -1),
        transfer_map,
        history,
        retard_index,
        retard_frac,
        retard_weight,
        z_kernel.T,
        x_kernel,
    )
    anywhere = pl.BlockSpec(memory_space=pl.ANY)
    kicked, field, deposit = pl.pallas_call(
        place,
        out_shape=shapes,
        in_specs=[vmem] * 3,
        out_specs=(anywhere,) * 3,
        scratch_shapes=[sem((3,))],
        cost_estimate=pl.CostEstimate(flops=0, bytes_accessed=10**5, transcendentals=0),
    )(*[pltpu.with_memory_space_constraint(r, pltpu.VMEM) for r in results])
    return kicked, jnp.swapaxes(field, 1, 2), jnp.swapaxes(deposit, 1, 2)


def solution(mesh):
    return jax.shard_map(
        local,
        mesh=mesh,
        in_specs=(
            P(None, ("dom", "hist")),
            P(("dom", "hist")),
            P(("dom", "hist")),
            P(("dom", "hist")),
            P(("dom", "hist")),
            P(),
            P("hist", None, "dom", None),
            P("hist"),
            P("hist"),
            P("hist"),
            P(None, "dom"),
            P(),
        ),
        out_specs=(P(None, ("dom", "hist")), P(None, "dom", "hist"), P(None, "dom", "hist")),
        check_vma=False,
    )
```

```python
import jax
import jax.numpy as jnp
from jax import lax
from jax.experimental import pallas as pl
from jax.experimental.pallas import tpu as pltpu
from jax.sharding import PartitionSpec as P

MESH = pl.DeviceIdType.MESH
F32 = jnp.float32
BF16 = jnp.bfloat16


def split(value):
    high = value.astype(BF16)
    return high, (value - high.astype(F32)).astype(BF16)


def dot_nn(a, b):
    return lax.dot_general(a, b, (((1,), (0,)), ((), ())), preferred_element_type=F32)


def dot_nt(a, b):
    return lax.dot_general(a, b, (((1,), (1,)), ((), ())), preferred_element_type=F32)


def dot_tn(a, b):
    return lax.dot_general(a, b, (((0,), (0,)), ((), ())), preferred_element_type=F32)


def kernel(
    coords_hbm, charge_hbm, row_hbm, block_hbm, offset_hbm, map_hbm, history_hbm, lag_hbm, frac_hbm,
    weight_hbm, z_hbm, x_hbm,
    kicked_ref, field_ref, deposit_ref,
    coords_ref, charge_ref, row_ref, block_ref, offset_ref, map_ref, lag_ref, frac_ref, weight_ref,
    history, x_full, z_own, near, x_high, x_low, z_high, z_low,
    a_send, a_recv, d_send, d_recv, e_send, e_recv, core_send, core_recv, ring_send, ring_recv,
    slab_t, column_hot, row_hot, pushed,
    load_sem, a_ssem, a_rsem, d_ssem, d_rsem, e_ssem, e_rsem, c_ssem, c_rsem, r_ssem, r_rsem,
    g_ssem, g_rsem, far_sem,
):
    hist = lax.axis_index("hist")
    dom = lax.axis_index("dom")
    z_low_at, plane = hist // 16, hist % 16
    z_high_at, core = dom // 2, dom % 2
    z_at = z_high_at * 4 + z_low_at

    plane_steps = sorted(
        [(a, b) for a in range(4) for b in range(4) if a or b],
        key=lambda step: -(min(step[0], 4 - step[0]) + min(step[1], 4 - step[1])),
    )
    plane_at = [lax.rem(plane // 4 + a, 4) * 4 + lax.rem(plane % 4 + b, 4) for a, b in plane_steps]
    plane_peers = [{"hist": z_low_at * 16 + at, "dom": dom} for at in plane_at]
    ring_steps = sorted(range(1, 16), key=lambda k: -min(k, 16 - k))
    ring_at = [lax.rem(z_at + k, 16) for k in ring_steps]
    ring_peers = [{"hist": (at % 4) * 16 + plane, "dom": (at // 4) * 2 + core} for at in ring_at]
    ring_near = [peer for k, peer in zip(ring_steps, ring_peers) if min(k, 16 - k) <= 4]
    ring_four = [peer for k, peer in zip(ring_steps, ring_peers) if min(k, 16 - k) == 4]
    low_at = [lax.rem(z_low_at + k, 4) for k in range(1, 4)]
    low_peers = [{"hist": at * 16 + plane, "dom": dom} for at in low_at]
    def stage(buffer, send_sem, recv_sem):
        return pltpu.make_async_remote_copy(
            src_ref=buffer, dst_ref=buffer, send_sem=send_sem, recv_sem=recv_sem,
            device_id=plane_peers[0], device_id_type=MESH,
        )

    a_stage = stage(a_recv, a_ssem, a_rsem)
    d_stage = stage(d_recv, d_ssem, d_rsem)
    e_stage = stage(e_recv, e_ssem, e_rsem)
    r_stage = stage(ring_recv, r_ssem, r_rsem)
    g_stage = stage(slab_t.at[0:15], g_ssem, g_rsem)
    sibling = {"hist": hist, "dom": z_high_at * 2 + (1 - core)}

    def load(index, source, target):
        copy = pltpu.make_async_copy(source, target, load_sem.at[index])
        copy.start()
        return copy

    load_history = load(0, history_hbm, history)
    load_steps = [load(1, lag_hbm, lag_ref), load(2, frac_hbm, frac_ref), load(3, weight_hbm, weight_ref)]
    load_x = load(4, x_hbm, x_full)
    barrier = pltpu.get_barrier_semaphore()
    for peer in plane_peers + ring_near + [sibling]:
        pl.semaphore_signal(barrier, inc=1, device_id=peer, device_id_type=MESH)

    load_z = load(5, z_hbm, z_own)
    load_particles = [
        load(6, coords_hbm, coords_ref), load(7, charge_hbm, charge_ref), load(8, row_hbm, row_ref),
        load(9, block_hbm, block_ref), load(10, offset_hbm, offset_ref), load(11, map_hbm, map_ref),
    ]

    lane = lax.broadcasted_iota(jnp.int32, (32, 128), 1)
    for copy in load_steps:
        copy.wait()
    load_history.wait()

    def source_rows(group, carry):
        comp = group // 2
        row = pl.multiple_of((group % 2) * 32, 32)
        row_out = pl.multiple_of(group * 32, 32)
        near_sum = [jnp.zeros((32, 128), F32) for _ in range(4)]
        far_sum = [jnp.zeros((32, 128), F32) for _ in range(4)]
        for t in range(8):
            lag = lag_ref[t]
            fraction = frac_ref[t]
            weight = weight_ref[t]
            near_weight = weight * (1.0 - fraction)
            far_weight = weight * fraction
            inside = lane >= lag
            before = jnp.zeros((32, 128), F32)
            for j in range(4):
                piece = history[t, comp, pl.ds(row, 32), 128 * j : 128 * (j + 1)].astype(F32)
                turned = pltpu.roll(piece, lag, 1)
                moved = jnp.where(inside, turned, before)
                before = turned
                near_sum[j] = near_sum[j] + near_weight * moved
                far_sum[j] = far_sum[j] + far_weight * moved
        before = jnp.zeros((32, 128), F32)
        for j in range(4):
            turned = pltpu.roll(far_sum[j], 1, 1)
            near[pl.ds(row_out, 32), 128 * j : 128 * (j + 1)] = near_sum[j] + jnp.where(
                lane >= 1, turned, before
            )
            before = turned
        return carry

    lax.fori_loop(0, 4, source_rows, 0)

    load_x.wait()
    x_high[...], x_low[...] = split(x_full[...])
    s_high, s_low = split(near[...])
    twice = dot_nn(jnp.concatenate([s_high, s_low], axis=0), x_high[...])
    spread = twice[:128] + twice[128:] + dot_nn(s_high, x_low[...])
    spread_t = spread.T.reshape(4, 16, 8, 128)
    for zc in range(4):
        a_send[:, zc] = spread_t[zc]

    pl.semaphore_wait(barrier, 24)
    for peer in ring_four:
        pl.semaphore_signal(far_sem, inc=1, device_id=peer, device_id_type=MESH)

    for k in range(1, 16):
        to = plane_at[k - 1]
        copy = pltpu.make_async_remote_copy(
            src_ref=a_send.at[to], dst_ref=a_recv.at[k - 1], send_sem=a_ssem,
            recv_sem=a_rsem, device_id=plane_peers[k - 1], device_id_type=MESH,
        )
        copy.start()

    load_z.wait()
    empty = jnp.zeros((64, 64), F32)
    for to in range(8):
        block = z_own[:, 64 * to : 64 * (to + 1)]
        pair = jnp.concatenate(
            [jnp.concatenate([block, empty], axis=1), jnp.concatenate([empty, block], axis=1)], axis=0
        )
        z_high[:, 128 * to : 128 * (to + 1)], z_low[:, 128 * to : 128 * (to + 1)] = split(pair)

    for copy in load_particles:
        copy.wait()
    for chunk in range(4):
        lanes = slice(512 * chunk, 512 * (chunk + 1))
        wide = [jnp.broadcast_to(coords_ref[i : i + 1, lanes], (6, 512)) for i in range(6)]
        total = jnp.broadcast_to(map_ref[:, 0:1], (6, 512))
        at = 1
        for i in range(6):
            total = total + map_ref[:, at : at + 1] * wide[i]
            at += 1
        for i in range(6):
            for j in range(i, 6):
                total = total + map_ref[:, at : at + 1] * (wide[i] * wide[j])
                at += 1
        for i in range(6):
            for j in range(i, 6):
                two = wide[i] * wide[j]
                for k in range(j, 6):
                    total = total + map_ref[:, at : at + 1] * (two * wide[k])
                    at += 1
        pushed[:, lanes] = total

    row = row_ref[...] - dom * 64
    first = jnp.concatenate([jnp.full((1, 128), block_ref[b], jnp.int32) for b in range(16)], axis=1)
    column = first + offset_ref[...]
    place = ((column >> 3) & 15) * 32 + (column >> 7) * 8 + (column & 7)
    charge = charge_ref[...]
    weights = [charge.astype(BF16).astype(F32), (charge * pushed[1:2, :]).astype(BF16).astype(F32)]
    row_iota = lax.broadcasted_iota(jnp.int32, (64, 2048), 0)
    here = row_iota == row
    for c in range(2):
        row_hot[64 * c : 64 * (c + 1), :] = jnp.where(here, weights[c], 0.0).astype(BF16)
    place_iota = lax.broadcasted_iota(jnp.int32, (64, 2048), 0)

    def deposit_rows(step, carry):
        at = pl.multiple_of(step * 64, 64)
        hot = jnp.where(place_iota == place - at, 1.0, 0.0).astype(BF16)
        column_hot[pl.ds(at, 64), :] = hot
        rows = dot_nt(hot, row_hot[...]).astype(BF16)
        d_send[2 * step] = rows[:32]
        d_send[2 * step + 1] = rows[32:]
        return carry

    lax.fori_loop(0, 8, deposit_rows, 0)

    a_stage.wait_recv()
    part = a_send[plane]
    for k in range(15):
        part = part + a_recv[k]
    p_high, p_low = split(part.reshape(32, 128))
    twice = dot_nn(jnp.concatenate([p_high, p_low], axis=0), z_high[...])
    terms = twice[:32] + twice[32:] + dot_nn(p_high, z_low[...])
    for to in range(8):
        core_send[to % 2, to // 2] = terms[:, 128 * to : 128 * (to + 1)]
    core_copy = pltpu.make_async_remote_copy(
        src_ref=core_send.at[1 - core], dst_ref=core_recv, send_sem=c_ssem, recv_sem=c_rsem,
        device_id=sibling, device_id_type=MESH,
    )
    core_copy.start()
    core_copy.wait_recv()
    ring_send[...] = (core_send[core] + core_recv[...]).astype(BF16)

    pl.semaphore_wait(far_sem, 2)
    for k in range(1, 16):
        copy = pltpu.make_async_remote_copy(
            src_ref=ring_send.at[ring_at[k - 1] // 4], dst_ref=ring_recv.at[k - 1],
            send_sem=r_ssem, recv_sem=r_rsem, device_id=ring_peers[k - 1],
            device_id_type=MESH,
        )
        copy.start()

    for k in range(1, 16):
        to = plane_at[k - 1]
        copy = pltpu.make_async_remote_copy(
            src_ref=d_send.at[to], dst_ref=d_recv.at[k - 1], send_sem=d_ssem,
            recv_sem=d_rsem, device_id=plane_peers[k - 1], device_id_type=MESH,
        )
        copy.start()

    r_stage.wait_recv()
    total = core_send[core, z_high_at] + core_recv[z_high_at]
    for k in range(15):
        total = total + ring_recv[k].astype(F32)
    slab_t[plane] = total.astype(BF16)
    for k in range(1, 16):
        copy = pltpu.make_async_remote_copy(
            src_ref=slab_t.at[plane], dst_ref=slab_t.at[plane], send_sem=g_ssem,
            recv_sem=g_rsem, device_id=plane_peers[k - 1], device_id_type=MESH,
        )
        copy.start()

    d_stage.wait_recv()
    part = d_send[plane].astype(F32)
    for k in range(15):
        part = part + d_recv[k].astype(F32)
    e_send[...] = part.reshape(4, 8, 128)
    for k in range(1, 4):
        copy = pltpu.make_async_remote_copy(
            src_ref=e_send.at[low_at[k - 1]], dst_ref=e_recv.at[k - 1], send_sem=e_ssem,
            recv_sem=e_rsem, device_id=low_peers[k - 1], device_id_type=MESH,
        )
        copy.start()

    own = jnp.where(z_low_at == 0, total[0:8], 0.0)
    for zc in range(1, 4):
        own = own + jnp.where(z_low_at == zc, total[8 * zc : 8 * (zc + 1)], 0.0)
    field_ref[0] = own[:, :64]
    field_ref[1] = own[:, 64:]
    e_stage.wait_recv()
    own = e_send[z_low_at] + e_recv[0] + e_recv[1] + e_recv[2]
    deposit_ref[0] = own[:, :64]
    deposit_ref[1] = own[:, 64:]
    kicked_ref[...] = pushed[...]

    for part in (a_stage, d_stage, e_stage, core_copy, r_stage):
        part.wait_send()

    g_stage.wait_recv()
    sampled = dot_tn(slab_t[...].reshape(512, 128), column_hot[...])
    longitudinal = jnp.sum(jnp.where(here, sampled[:64], 0.0), axis=0, keepdims=True)
    transverse = jnp.sum(jnp.where(here, sampled[64:], 0.0), axis=0, keepdims=True)
    kicked_ref[5:6, :] = pushed[5:6, :] + 0.5 * longitudinal
    kicked_ref[1:2, :] = pushed[1:2, :] + 0.5 * transverse

    g_stage.wait_send()


def place(kicked_in, field_in, deposit_in, kicked_ref, field_ref, deposit_ref, sems):
    copies = [
        pltpu.make_async_copy(kicked_in, kicked_ref, sems.at[0]),
        pltpu.make_async_copy(field_in, field_ref, sems.at[1]),
        pltpu.make_async_copy(deposit_in, deposit_ref, sems.at[2]),
    ]
    for copy in copies:
        copy.start()
    for copy in copies:
        copy.wait()


def local(
    coords, charge, row_index, block_col, col_offset, transfer_map, history, retard_index, retard_frac,
    retard_weight, z_kernel, x_kernel,
):
    vmem = pl.BlockSpec(memory_space=pltpu.VMEM)
    hbm = pl.BlockSpec(memory_space=pltpu.HBM)
    sem = pltpu.SemaphoreType.DMA
    shapes = (
        jax.ShapeDtypeStruct((6, 2048), F32),
        jax.ShapeDtypeStruct((2, 8, 64), F32),
        jax.ShapeDtypeStruct((2, 8, 64), F32),
    )
    results = pl.pallas_call(
        kernel,
        out_shape=tuple(pltpu.VMEM(shape.shape, shape.dtype) for shape in shapes),
        in_specs=[hbm] * 12,
        out_specs=(vmem, vmem, vmem),
        scratch_shapes=[
            pltpu.VMEM((6, 2048), F32),
            pltpu.VMEM((1, 2048), F32),
            pltpu.VMEM((1, 2048), jnp.int32),
            pltpu.SMEM((16,), jnp.int32),
            pltpu.VMEM((1, 2048), jnp.int32),
            pltpu.VMEM((6, 84), F32),
            pltpu.SMEM((8,), jnp.int32),
            pltpu.SMEM((8,), F32),
            pltpu.SMEM((8,), F32),
            pltpu.VMEM((8, 2, 64, 512), BF16),
            pltpu.VMEM((512, 512), F32),
            pltpu.VMEM((64, 512), F32),
            pltpu.VMEM((128, 512), F32),
            pltpu.VMEM((512, 512), BF16),
            pltpu.VMEM((512, 512), BF16),
            pltpu.VMEM((128, 1024), BF16),
            pltpu.VMEM((128, 1024), BF16),
            pltpu.VMEM((16, 4, 8, 128), F32),
            pltpu.VMEM((15, 4, 8, 128), F32),
            pltpu.VMEM((16, 32, 128), BF16),
            pltpu.VMEM((15, 32, 128), BF16),
            pltpu.VMEM((4, 8, 128), F32),
            pltpu.VMEM((3, 8, 128), F32),
            pltpu.VMEM((2, 4, 32, 128), F32),
            pltpu.VMEM((4, 32, 128), F32),
            pltpu.VMEM((4, 32, 128), BF16),
            pltpu.VMEM((15, 32, 128), BF16),
            pltpu.VMEM((16, 32, 128), BF16),
            pltpu.VMEM((512, 2048), BF16),
            pltpu.VMEM((128, 2048), BF16),
            pltpu.VMEM((6, 2048), F32),
            sem((12,)),
            sem, sem,
            sem, sem,
            sem, sem,
            sem, sem,
            sem, sem,
            sem, sem, pltpu.SemaphoreType.REGULAR,
        ],
        compiler_params=pltpu.CompilerParams(
            collective_id=0, has_side_effects=True, vmem_limit_bytes=58 * 1024 * 1024
        ),
        cost_estimate=pl.CostEstimate(flops=10**9, bytes_accessed=4 * 10**6, transcendentals=0),
    )(
        coords,
        charge.reshape(1, -1),
        row_index.reshape(1, -1),
        block_col,
        col_offset.reshape(1, -1),
        transfer_map,
        history,
        retard_index,
        retard_frac,
        retard_weight,
        z_kernel.T,
        x_kernel,
    )
    anywhere = pl.BlockSpec(memory_space=pl.ANY)
    kicked, field, deposit = pl.pallas_call(
        place,
        out_shape=shapes,
        in_specs=[vmem] * 3,
        out_specs=(anywhere,) * 3,
        scratch_shapes=[sem((3,))],
        cost_estimate=pl.CostEstimate(flops=0, bytes_accessed=10**5, transcendentals=0),
    )(*[pltpu.with_memory_space_constraint(r, pltpu.VMEM) for r in results])
    return kicked, jnp.swapaxes(field, 1, 2), jnp.swapaxes(deposit, 1, 2)


def solution(mesh):
    return jax.shard_map(
        local,
        mesh=mesh,
        in_specs=(
            P(None, ("dom", "hist")),
            P(("dom", "hist")),
            P(("dom", "hist")),
            P(("dom", "hist")),
            P(("dom", "hist")),
            P(),
            P("hist", None, "dom", None),
            P("hist"),
            P("hist"),
            P("hist"),
            P(None, "dom"),
            P(),
        ),
        out_specs=(P(None, ("dom", "hist")), P(None, "dom", "hist"), P(None, "dom", "hist")),
        check_vma=False,
    )
```
